32 devices in a mesh: outer: 8 (over z, core), inner: 4 (over y, x).
Axes of the slice: x: 2, y: 2, z: 4, core: 2. Of those that a mesh axis runs over, the one named last changes fastest.
Arguments:
- queries: bfloat16 [12288, 1536], P(('outer', 'inner')), may hold values from -6 to 6
- key_vectors: bfloat16 [12288, 1536], P(('outer', 'inner')), may hold values from -6 to 6
- value_vectors: bfloat16 [12288, 1536], P(('outer', 'inner')), may hold values from -6 to 6
- write_gate: float32 [12, 12288], P(None, ('outer', 'inner')), may hold values from 0.05 to 1
- ridge_term: float32 [12], replicated, may hold values from 0.25 to 4
- segment_ids: int32 [12288], P(('outer', 'inner')), may hold values from 0 to 15, never falling along the last dimension, each value on 1 to 1536 neighbouring positions
Outputs:
- mixed_heads: bfloat16 [12288, 1536], P(('outer', 'inner'))
The draws below stay inside these ranges and needn't reach their ends.
Inputs may be any that keep to these rules, and one draw needn't show every extreme that they name: `segment_ids`: segment ids never fall along the tokens; each of the 16 documents spans 1 to 1536 tokens, one exactly 1536.
All inputs are finite; a program needn't handle non-finite values.
Results may differ from the reference program's by a relative error of at most 0.001.
Values sent between devices are 32-bit elements; how exact they have to be, the bound alone decides.
A program may use at most 64 MiB of HBM per device.

```python
import math
import jax
import jax.numpy as jnp
import numpy as np
from jax import lax

HEADS = 12
DH = 128
STRETCH = 128
ITERS = 4
TOKENS = 12288
DOC_MOST = 1536
DOCS = 16


def level_of(rng, extent, pieces, least, largest):
    def one(axis_at, shards_of):
        draws = jax.random.uniform(jax.random.fold_in(jax.random.fold_in(rng, 6), axis_at), (shards_of,), jnp.float32, least / len(pieces), largest / len(pieces))
        return jnp.repeat(jnp.exp(draws), extent[axis_at] // shards_of).reshape((-1,) + (1,) * (len(extent) - axis_at - 1))

    factor_of = one(*pieces[0])
    for cut in pieces[1:]:
        factor_of = factor_of * one(*cut)
    return factor_of


def profile(count, total, reach, lean):
    loads = [(1 << 20) // math.isqrt(rank ** lean) + 1 for rank in range(2, count + 1)]
    spare, given = total - reach - (count - 1), [1] * (count - 1)
    while spare > 0:
        candidates = [i for i in range(count - 1) if given[i] < reach]
        pool, left = sum([loads[i] for i in candidates]), spare
        for i in candidates:
            more = min(reach - given[i], max(1, left * loads[i] // pool), spare)
            given[i] = given[i] + more
            spare = spare - more
    return np.array([reach] + given)


def uneven(own_key, amount, total, bound, skew):
    if amount == 2:
        one = jax.random.randint(own_key, (), max(1, total - bound), min(bound, total - 1) + 1)
        return jnp.stack([one, total - one])
    sizes = jnp.asarray(profile(amount, total, bound, skew), jnp.int32)
    pairs = (amount - 1) // 2
    giver, taker = sizes[1:1 + 2 * pairs:2], sizes[2:2 + 2 * pairs:2]
    slack = jnp.minimum(giver - 1, bound - taker)
    passed = jax.random.randint(jax.random.fold_in(own_key, 1), (pairs,), 0, 1 << 20) % (slack + 1)
    sizes = sizes.at[1:1 + 2 * pairs:2].set(giver - passed).at[2:2 + 2 * pairs:2].set(taker + passed)
    return sizes[jax.random.permutation(jax.random.fold_in(own_key, 2), amount)]


def centred(rng, dims, scale, limit, split=(), dtype=jnp.bfloat16):
    drawn = scale * jax.random.normal(rng, dims, jnp.float32)
    if split:
        drawn = drawn * level_of(rng, dims, split, -0.22, 0.18)
    return jnp.clip(drawn, -limit, limit).astype(dtype)


def setup_inputs(seed: int = 0) -> dict:
    splits = jax.random.split(jax.random.key(seed), 7)
    queries = centred(splits[0], (TOKENS, HEADS * DH), 1.0, 6.0, ((0, 32),))
    key_vectors = centred(splits[1], (TOKENS, HEADS * DH), 1.0, 6.0, ((0, 32),))
    value_vectors = centred(splits[2], (TOKENS, HEADS * DH), 1.0, 6.0, ((0, 32),))
    write_gate = jnp.clip(jnp.exp(math.log(1.0) - 2.9957323 * jax.random.uniform(splits[3], (HEADS, TOKENS), jnp.float32) ** level_of(splits[3], (HEADS, TOKENS), ((1, 32),), -0.2, 0.2)), 0.05, 1.0)
    ridge_term = jnp.clip(jnp.exp(jax.random.uniform(splits[4], (HEADS,), jnp.float32, math.log(0.25), math.log(4.0))), 0.25, 4.0)
    segment_ids = jnp.searchsorted(jnp.cumsum(uneven(splits[5], DOCS, TOKENS, DOC_MOST, 2)), jnp.arange(TOKENS), side="right").astype(jnp.int32)
    return {"queries": queries, "key_vectors": key_vectors, "value_vectors": value_vectors, "write_gate": write_gate, "ridge_term": ridge_term, "segment_ids": segment_ids}


highest = lax.Precision.HIGHEST

def normed_heads(raw, heads):
    rows = raw.shape[0]
    values = raw.astype(jnp.float32).reshape(rows, heads, -1).transpose(1, 0, 2)
    return values * lax.rsqrt(lax.optimization_barrier(jnp.sum(values * values, axis=-1, keepdims=True)) + 1e-06)

def block_step(carry, block, ridge_term):
    gram, memory, previous = carry
    query_raw, key_raw, value_raw, gate_rows, seg_rows = block
    heads = ridge_term.shape[0]
    query_rows = normed_heads(query_raw, heads)
    key_rows = normed_heads(key_raw, heads)
    value_rows = value_raw.astype(jnp.float32).reshape(value_raw.shape[0], heads, -1).transpose(1, 0, 2)
    length = seg_rows.shape[0]
    keep = (seg_rows == previous).astype(jnp.float32)[None, :, None]
    order = jnp.arange(length)
    causal = (seg_rows[:, None] == seg_rows[None, :]) & (order[None, :] <= order[:, None])
    weights = causal.astype(jnp.float32)[None] * gate_rows[:, None, :]

    def apply_gram(direction):
        carried = jnp.einsum('hte,hed->htd', direction, gram, precision=highest) * keep
        scores = jnp.einsum('htd,hsd->hts', direction, key_rows, precision=highest) * weights
        inside = jnp.einsum('hts,hsd->htd', scores, key_rows, precision=highest)
        return carried + inside + ridge_term[:, None, None] * direction
    solved = jnp.zeros_like(query_rows)
    residual = query_rows
    direction = query_rows
    resid_sq = lax.optimization_barrier(jnp.sum(residual * residual, axis=-1, keepdims=True))
    for sweep in range(ITERS):
        image = apply_gram(direction)
        step_size = resid_sq / lax.optimization_barrier(jnp.sum(direction * image, axis=-1, keepdims=True))
        solved = solved + step_size * direction
        residual = residual - step_size * image
        fresh_sq = lax.optimization_barrier(jnp.sum(residual * residual, axis=-1, keepdims=True))
        direction = residual + fresh_sq / resid_sq * direction
        resid_sq = fresh_sq
    carried_out = jnp.einsum('htk,hvk->htv', solved, memory, precision=highest) * keep
    scores = jnp.einsum('htd,hsd->hts', solved, key_rows, precision=highest) * weights
    inside_out = jnp.einsum('hts,hsv->htv', scores, value_rows, precision=highest)
    result = (carried_out + inside_out).transpose(1, 0, 2).reshape(length, -1).astype(jnp.bfloat16)
    last_id = seg_rows[length - 1]
    stay = (last_id == previous).astype(jnp.float32)
    tail = (seg_rows == last_id).astype(jnp.float32)[None, :] * gate_rows
    key_tail = key_rows * tail[:, :, None]
    gram_next = stay * gram + jnp.einsum('hsk,hsl->hkl', key_tail, key_rows, precision=highest)
    memory_next = stay * memory + jnp.einsum('hsv,hsk->hvk', value_rows * tail[:, :, None], key_rows, precision=highest)
    return ((gram_next, memory_next, last_id), result)

def reference(queries, key_vectors, value_vectors, write_gate, ridge_term, segment_ids):
    blocks = TOKENS // STRETCH
    width = queries.shape[1]
    heads = ridge_term.shape[0]
    head_size = width // heads
    gate_blocks = write_gate.reshape(heads, blocks, STRETCH).transpose(1, 0, 2)
    xs = (queries.reshape(blocks, STRETCH, width), key_vectors.reshape(blocks, STRETCH, width), value_vectors.reshape(blocks, STRETCH, width), gate_blocks, segment_ids.reshape(blocks, STRETCH))
    zeros = jnp.zeros((heads, head_size, head_size), jnp.float32)
    init = (zeros, zeros, segment_ids[0])
    final, outputs = lax.scan(lambda carry, block: block_step(carry, block, ridge_term), init, xs)
    return outputs.reshape(TOKENS, width)
```

```python
import functools

import jax
import jax.numpy as jnp
from jax import lax
from jax.experimental import pallas as pl
from jax.experimental.pallas import tpu as pltpu
from jax.sharding import PartitionSpec as P

STRETCH = 128
ITERS = 4
LAG = 2
MESH = pl.DeviceIdType.MESH
F32 = jnp.float32
BF16 = jnp.bfloat16


def split(x):
    hi = x.astype(BF16)
    return hi, (x - hi.astype(F32)).astype(BF16)


def mm(a, b):
    return jnp.dot(a, b, preferred_element_type=F32)


def same(a, b):
    return (a == b).astype(F32)


def kernel(
    sizes, q_ref, k_ref, v_ref, gate_ref, ridge_ref, seg_ref, o_ref,
    causal, keep, kt_buf, gram_row, memory_row, part,
    local, got1, pair, got2, suffix, got3, id_out, id_in,
    send1, recv1, send2, recv2, send3, recv3, id_send, id_recv,
):
    outer, inner = sizes
    devices = outer * inner
    heads = gate_ref.shape[0]
    blocks = q_ref.shape[0] // STRETCH
    me = lax.axis_index("outer") * inner + lax.axis_index("inner")
    spot = me % 4
    odd_i, top_i = spot % 2, spot // 2

    def place(index):
        return (index // inner, index % inner)

    across1 = place(me + 1 - 2 * odd_i)
    across2 = place(me + 2 - 4 * top_i)
    after = place((me + 4) % devices)
    before = place((me + devices - 4) % devices)

    barrier = pltpu.get_barrier_semaphore()
    for target in (across1, across2, before):
        pl.semaphore_signal(barrier, inc=1, device_id=target, device_id_type=MESH)
    pl.semaphore_wait(barrier, 3)

    def exchange(src, dst, sender, receiver, target):
        return pltpu.make_async_remote_copy(
            src_ref=src, dst_ref=dst, send_sem=sender, recv_sem=receiver,
            device_id=target, device_id_type=MESH,
        )

    def phase1(h):
        return exchange(local.at[h], got1.at[h], send1.at[h], recv1.at[h], across1)

    def phase2(h):
        return exchange(pair.at[h], got2.at[h], send2.at[h], recv2.at[h], across2)

    def phase3(h):
        return exchange(suffix.at[h], got3.at[h], send3.at[h], recv3.at[h], after)

    def id_phase(p):
        target = (across1, across2, after)[p]
        return exchange(id_out.at[p], id_in.at[p], id_send.at[p], id_recv.at[p], target)

    seg = seg_ref[...].astype(F32)
    first = seg[0:1, 0:1]
    rows = [seg[b:b + 1, :] for b in range(blocks)]
    last = [seg[b:b + 1, STRETCH - 1:STRETCH] for b in range(blocks)]

    id_out[0] = jnp.broadcast_to(last[-1], (8, 128))
    id_phase(0).start()

    odd, top = odd_i.astype(F32), top_i.astype(F32)
    for b in range(blocks):
        grid_rows = jnp.broadcast_to(rows[b], (STRETCH, STRETCH))
        grid_cols = grid_rows.T
        down = lax.broadcasted_iota(jnp.int32, (STRETCH, STRETCH), 0)
        over = lax.broadcasted_iota(jnp.int32, (STRETCH, STRETCH), 1)
        causal[b] = jnp.where(over <= down, same(grid_rows, grid_cols), 0.0)
        keep[b] = same(grid_cols, first if b == 0 else last[b - 1]).astype(BF16)

    tails = [same(rows[b], last[b]) for b in range(blocks)]

    def columns(h):
        return pl.ds(pl.multiple_of(h * 128, 128), 128)

    def span(b):
        return slice(b * STRETCH, (b + 1) * STRETCH)

    def gather_local(h, carry):
        total = jnp.zeros((256, 128), F32)
        for b in range(blocks):
            keys = k_ref[span(b), columns(h)]
            values = v_ref[span(b), columns(h)]
            wide = keys.astype(F32).T
            kt_buf[h, b] = wide.astype(BF16)
            scale = lax.rsqrt(jnp.sum(wide * wide, axis=0, keepdims=True) + 1e-06)
            w1 = memory_row[h, b] * scale
            w2 = w1 * scale
            memory_row[h, b] = w1
            gram_row[h, b] = w2
            ghi, glo = split(wide * (w2 * tails[b]))
            mhi, mlo = split(wide * (w1 * tails[b]))
            gram = mm(jnp.concatenate([ghi, glo], 1), jnp.concatenate([keys, keys], 0))
            memory = mm(jnp.concatenate([mhi, mlo], 1), jnp.concatenate([values, values], 0))
            both = jnp.concatenate([gram, memory], 0)
            if b < blocks - 1:
                part[h, b] = both
            total = total + same(last[b], last[-1]) * both
        local[h] = total
        phase1(h).start()
        return carry

    for h in range(heads):
        for b in range(blocks):
            memory_row[h, b] = gate_ref[h:h + 1, span(b)]
    lax.fori_loop(0, heads, gather_local, 0)

    id_phase(0).wait_recv()
    other_last = id_in[0][0:1, 0:1]
    equal = same(last[-1], other_last)
    pair_local = odd + (1.0 - odd) * equal
    pair_got = (1.0 - odd) + odd * equal
    pair_id = odd * last[-1] + (1.0 - odd) * other_last
    id_out[1] = jnp.broadcast_to(pair_id, (8, 128))
    id_phase(1).start()
    id_phase(1).wait_recv()
    far_id = id_in[1][0:1, 0:1]
    base = top + (1.0 - top) * same(pair_id, far_id)
    suffix_local = base * (odd + (1.0 - odd) * pair_local)
    suffix_got = base * (1.0 - odd) * pair_got
    id_out[2] = jnp.broadcast_to(top * pair_id + (1.0 - top) * far_id, (8, 128))
    id_phase(2).start()
    id_phase(2).wait_recv()
    in1 = odd * same(other_last, first)
    in2 = top * same(far_id, first)
    in3 = same(id_in[2][0:1, 0:1], first)

    def solve(h):
        ridge = ridge_ref[h]
        state = in1 * got1[h] + in2 * got2[h] + in3 * got3[h]
        keys, lifts, mems, kts, weights, masks = [], [], [], [], [], []
        xs, rs, ds, sqs = [], [], [], []
        for b in range(blocks):
            if b > 0:
                previous = first if b == 1 else last[b - 2]
                state = part[h, b - 1] + same(last[b - 1], previous) * state
            hi, lo = split(state)
            k = k_ref[span(b), columns(h)]
            v = v_ref[span(b), columns(h)]
            lifts.append(jnp.concatenate([k, k, hi[:128], hi[:128], lo[:128]], 0))
            mems.append(jnp.concatenate([v, v, hi[128:], hi[128:], lo[128:]], 0))
            kt = kt_buf[h, b]
            kts.append(jnp.concatenate([kt, kt], 0))
            weights.append(causal[b] * gram_row[h, b])
            q = q_ref[span(b), columns(h)].astype(F32)
            q = q * lax.rsqrt(jnp.sum(q * q, axis=-1, keepdims=True) + 1e-06)
            xs.append(jnp.zeros_like(q))
            rs.append(q)
            ds.append(q)
            sqs.append(jnp.sum(q * q, axis=-1, keepdims=True))

        def apply(b, d, weight, lift):
            hi, lo = split(d)
            scores = mm(jnp.concatenate([hi, lo], 1), kts[b]) * weight
            shi, slo = split(scores)
            mask = keep[b]
            khi, klo = hi * mask, lo * mask
            return mm(jnp.concatenate([shi, slo, khi, klo, khi], 1), lift)

        for sweep in range(ITERS):
            for b in range(blocks):
                d = ds[b]
                image = apply(b, d, weights[b], lifts[b]) + ridge * d
                size = sqs[b] / jnp.sum(d * image, axis=-1, keepdims=True)
                xs[b] = xs[b] + size * d
                if sweep < ITERS - 1:
                    rs[b] = rs[b] - size * image
                    fresh = jnp.sum(rs[b] * rs[b], axis=-1, keepdims=True)
                    ds[b] = rs[b] + fresh / sqs[b] * d
                    sqs[b] = fresh
        for b in range(blocks):
            out = apply(b, xs[b], causal[b] * memory_row[h, b], mems[b])
            o_ref[span(b), columns(h)] = out.astype(BF16)

    def stage(t, carry):
        @pl.when(t < heads)
        def _():
            phase1(t).wait_recv()
            pair[t] = pair_local * local[t] + pair_got * got1[t]
            phase2(t).start()

        @pl.when(t >= LAG)
        def _():
            phase3(t - LAG).wait_recv()
            solve(t - LAG)

        @pl.when(t < heads)
        def _():
            phase2(t).wait_recv()
            suffix[t] = (
                (1.0 - top) * got2[t] + suffix_local * local[t] + suffix_got * got1[t]
            )
            phase3(t).start()

        return carry

    lax.fori_loop(0, heads + LAG, stage, 0)

    def drain(h, carry):
        phase1(h).wait_send()
        phase2(h).wait_send()
        phase3(h).wait_send()
        return carry

    lax.fori_loop(0, heads, drain, 0)
    for p in range(3):
        id_phase(p).wait_send()


def body(sizes, queries, key_vectors, value_vectors, write_gate, ridge_term, segment_ids):
    tokens, width = queries.shape
    heads = ridge_term.shape[0]
    blocks = tokens // STRETCH
    vmem = pl.BlockSpec(memory_space=pltpu.VMEM)
    smem = pl.BlockSpec(memory_space=pltpu.SMEM)
    state = pltpu.VMEM((heads, 256, 128), F32)
    return pl.pallas_call(
        functools.partial(kernel, sizes),
        out_shape=jax.ShapeDtypeStruct((tokens, width), BF16),
        in_specs=[vmem, vmem, vmem, vmem, smem, vmem],
        out_specs=vmem,
        scratch_shapes=[
            pltpu.VMEM((blocks, STRETCH, STRETCH), F32),
            pltpu.VMEM((blocks, STRETCH, STRETCH), BF16),
            pltpu.VMEM((heads, blocks, 128, STRETCH), BF16),
            pltpu.VMEM((heads, blocks, 1, STRETCH), F32),
            pltpu.VMEM((heads, blocks, 1, STRETCH), F32),
            pltpu.VMEM((heads, blocks - 1, 256, 128), F32),
            state, state, state, state, state, state,
            pltpu.VMEM((3, 8, 128), F32),
            pltpu.VMEM((3, 8, 128), F32),
        ] + [pltpu.SemaphoreType.DMA((heads,))] * 6 + [pltpu.SemaphoreType.DMA((3,))] * 2,
        compiler_params=pltpu.CompilerParams(
            collective_id=0, has_side_effects=True, vmem_limit_bytes=50 * 1024 * 1024
        ),
        cost_estimate=pl.CostEstimate(
            flops=6_000_000_000, bytes_accessed=6_000_000, transcendentals=0
        ),
    )(
        queries, key_vectors, value_vectors, write_gate, ridge_term,
        segment_ids.reshape(blocks, STRETCH),
    )


def solution(mesh):
    sizes = (mesh.shape["outer"], mesh.shape["inner"])
    return jax.shard_map(
        functools.partial(body, sizes),
        mesh=mesh,
        in_specs=(
            P(("outer", "inner"), None),
            P(("outer", "inner"), None),
            P(("outer", "inner"), None),
            P(None, ("outer", "inner")),
            P(),
            P(("outer", "inner")),
        ),
        out_specs=P(("outer", "inner"), None),
        check_vma=False,
    )
```

```python
import functools

import jax
import jax.numpy as jnp
from jax import lax
from jax.experimental import pallas as pl
from jax.experimental.pallas import tpu as pltpu
from jax.sharding import PartitionSpec as P

STRETCH = 128
ITERS = 4
LAG = 2
MESH = pl.DeviceIdType.MESH
F32 = jnp.float32
BF16 = jnp.bfloat16


def split(x):
    hi = x.astype(BF16)
    return hi, (x - hi.astype(F32)).astype(BF16)


def mm(a, b):
    return jnp.dot(a, b, preferred_element_type=F32)


def same(a, b):
    return (a == b).astype(F32)


def kernel(
    sizes, q_far, k_far, v_far, gate_far, ridge_ref, seg_far, o_ref,
    q_ref, k_ref, v_ref, gate_ref, seg_ref, load_sem,
    causal, causal_t, keep, kt_buf, gram_row, memory_row, part,
    local, got1, pair, got2, suffix, got3, id_out, id_in,
    send1, recv1, send2, recv2, send3, recv3, id_send, id_recv,
):
    loads = [
        pltpu.make_async_copy(far, near, load_sem.at[i])
        for i, (far, near) in enumerate((
            (seg_far, seg_ref), (k_far, k_ref), (gate_far, gate_ref),
            (v_far, v_ref), (q_far, q_ref),
        ))
    ]
    for load in loads:
        load.start()
    outer, inner = sizes
    devices = outer * inner
    heads = gate_ref.shape[0]
    blocks = q_ref.shape[0] // STRETCH
    me = lax.axis_index("outer") * inner + lax.axis_index("inner")
    spot = me % 4
    odd_i, top_i = spot % 2, spot // 2

    def place(index):
        return (index // inner, index % inner)

    across1 = place(me + 1 - 2 * odd_i)
    across2 = place(me + 2 - 4 * top_i)
    after = place((me + 4) % devices)
    before = place((me + devices - 4) % devices)

    barrier = pltpu.get_barrier_semaphore()
    for target in (across1, across2, before):
        pl.semaphore_signal(barrier, inc=1, device_id=target, device_id_type=MESH)
    pl.semaphore_wait(barrier, 3)

    def exchange(src, dst, sender, receiver, target):
        return pltpu.make_async_remote_copy(
            src_ref=src, dst_ref=dst, send_sem=sender, recv_sem=receiver,
            device_id=target, device_id_type=MESH,
        )

    def phase1(h):
        return exchange(local.at[h], got1.at[h], send1.at[h], recv1.at[h], across1)

    def phase2(h):
        return exchange(pair.at[h], got2.at[h], send2.at[h], recv2.at[h], across2)

    def phase3(h):
        return exchange(suffix.at[h], got3.at[h], send3.at[h], recv3.at[h], after)

    def id_phase(p):
        target = (across1, across2, after)[p]
        return exchange(id_out.at[p], id_in.at[p], id_send.at[p], id_recv.at[p], target)

    loads[0].wait()
    seg = seg_ref[...].astype(F32)
    first = seg[0:1, 0:1]
    rows = [seg[b:b + 1, :] for b in range(blocks)]
    last = [seg[b:b + 1, STRETCH - 1:STRETCH] for b in range(blocks)]

    id_out[0] = jnp.broadcast_to(last[-1], (8, 128))
    id_phase(0).start()

    odd, top = odd_i.astype(F32), top_i.astype(F32)
    for b in range(blocks):
        grid_rows = jnp.broadcast_to(rows[b], (STRETCH, STRETCH))
        grid_cols = grid_rows.T
        down = lax.broadcasted_iota(jnp.int32, (STRETCH, STRETCH), 0)
        over = lax.broadcasted_iota(jnp.int32, (STRETCH, STRETCH), 1)
        causal[b] = jnp.where(over <= down, same(grid_rows, grid_cols), 0.0)
        causal_t[b] = causal[b].T
        keep[b] = same(grid_cols, first if b == 0 else last[b - 1]).astype(BF16)

    tails = [same(rows[b], last[b]) for b in range(blocks)]

    def columns(h):
        return pl.ds(pl.multiple_of(h * 128, 128), 128)

    def span(b):
        return slice(b * STRETCH, (b + 1) * STRETCH)

    def gather_local(h, carry):
        total = jnp.zeros((256, 128), F32)
        for b in range(blocks):
            keys = k_ref[span(b), columns(h)]
            values = v_ref[span(b), columns(h)]
            wide = keys.astype(F32).T
            kt_buf[h, b] = wide.astype(BF16)
            scale = lax.rsqrt(jnp.sum(wide * wide, axis=0, keepdims=True) + 1e-06)
            w1 = memory_row[h, b] * scale
            w2 = w1 * scale
            memory_row[h, b] = w1
            gram_row[h, b] = w2
            ghi, glo = split(wide * (w2 * tails[b]))
            mhi, mlo = split(wide * (w1 * tails[b]))
            gram = mm(jnp.concatenate([ghi, glo], 1), jnp.concatenate([keys, keys], 0))
            memory = mm(jnp.concatenate([mhi, mlo], 1), jnp.concatenate([values, values], 0))
            both = jnp.concatenate([gram, memory], 0)
            if b < blocks - 1:
                part[h, b] = both
            total = total + same(last[b], last[-1]) * both
        local[h] = total
        phase1(h).start()
        return carry

    for load in loads[1:4]:
        load.wait()
    for h in range(heads):
        for b in range(blocks):
            memory_row[h, b] = gate_ref[h:h + 1, span(b)]
    lax.fori_loop(0, heads, gather_local, 0)

    loads[4].wait()
    id_phase(0).wait_recv()
    other_last = id_in[0][0:1, 0:1]
    equal = same(last[-1], other_last)
    pair_local = odd + (1.0 - odd) * equal
    pair_got = (1.0 - odd) + odd * equal
    pair_id = odd * last[-1] + (1.0 - odd) * other_last
    id_out[1] = jnp.broadcast_to(pair_id, (8, 128))
    id_phase(1).start()
    id_phase(1).wait_recv()
    far_id = id_in[1][0:1, 0:1]
    base = top + (1.0 - top) * same(pair_id, far_id)
    suffix_local = base * (odd + (1.0 - odd) * pair_local)
    suffix_got = base * (1.0 - odd) * pair_got
    id_out[2] = jnp.broadcast_to(top * pair_id + (1.0 - top) * far_id, (8, 128))
    id_phase(2).start()
    id_phase(2).wait_recv()
    in1 = odd * same(other_last, first)
    in2 = top * same(far_id, first)
    in3 = same(id_in[2][0:1, 0:1], first)

    def solve(h):
        ridge = ridge_ref[h]
        every = range(blocks)
        state = in1 * got1[h] + in2 * got2[h] + in3 * got3[h]
        mems, firsts, lows, seconds, weights, held = [], [], [], [], [], []
        xs, rs, ds, sqs = [], [], [], []
        for b in every:
            if b > 0:
                previous = first if b == 1 else last[b - 2]
                state = part[h, b - 1] + same(last[b - 1], previous) * state
            hi, lo = split(state)
            k = k_ref[span(b), columns(h)]
            v = v_ref[span(b), columns(h)]
            kt = kt_buf[h, b]
            firsts.append(jnp.concatenate(
                [jnp.concatenate([k, k], 1), jnp.concatenate([hi[:128], hi[:128]], 1)], 0
            ))
            lows.append(lo[:128])
            seconds.append(jnp.concatenate([kt, kt], 1))
            mems.append(jnp.concatenate([v, v, hi[128:], hi[128:], lo[128:]], 0))
            column = jnp.broadcast_to(gram_row[h, b], (8, STRETCH)).T[:, 0:1]
            weights.append(causal_t[b] * column)
            held.append(same(rows[b], first if b == 0 else last[b - 1]))
            q = q_ref[span(b), columns(h)].astype(F32).T
            q = q * lax.rsqrt(jnp.sum(q * q, axis=0, keepdims=True) + 1e-06)
            rs.append(q)
            ds.append(q)
            sqs.append(jnp.sum(q * q, axis=0, keepdims=True))

        for sweep in range(ITERS):
            cuts = [split(ds[b]) for b in every]
            raised = [mm(firsts[b], jnp.concatenate(cuts[b], 0)) for b in every]
            lowered = [mm(lows[b], cuts[b][0]) for b in every]
            scores = [split(raised[b][:128] * weights[b]) for b in every]
            inside = [mm(seconds[b], jnp.concatenate(scores[b], 0)) for b in every]
            for b in every:
                d = ds[b]
                image = inside[b] + held[b] * (raised[b][128:] + lowered[b]) + ridge * d
                size = sqs[b] / jnp.sum(d * image, axis=0, keepdims=True)
                if sweep == 0:
                    xs.append(size * d)
                else:
                    xs[b] = xs[b] + size * d
                if sweep < ITERS - 1:
                    rs[b] = rs[b] - size * image
                    fresh = jnp.sum(rs[b] * rs[b], axis=0, keepdims=True)
                    ds[b] = rs[b] + fresh / sqs[b] * d
                    sqs[b] = fresh
        cuts = [split(xs[b].T) for b in every]
        scores = []
        for b in every:
            kt = kt_buf[h, b]
            scores.append(mm(jnp.concatenate(cuts[b], 1), jnp.concatenate([kt, kt], 0)))
        for b in every:
            shi, slo = split(scores[b] * (causal[b] * memory_row[h, b]))
            hi, lo = cuts[b]
            mask = keep[b]
            khi, klo = hi * mask, lo * mask
            out = mm(jnp.concatenate([shi, slo, khi, klo, khi], 1), mems[b])
            o_ref[span(b), columns(h)] = out.astype(BF16)

    def stage(t, carry):
        @pl.when(t < heads)
        def _():
            phase1(t).wait_recv()
            pair[t] = pair_local * local[t] + pair_got * got1[t]
            phase2(t).start()

        @pl.when(t >= LAG)
        def _():
            phase3(t - LAG).wait_recv()
            solve(t - LAG)

        @pl.when(t < heads)
        def _():
            phase2(t).wait_recv()
            suffix[t] = (
                (1.0 - top) * got2[t] + suffix_local * local[t] + suffix_got * got1[t]
            )
            phase3(t).start()

        return carry

    lax.fori_loop(0, heads + LAG, stage, 0)

    def drain(h, carry):
        phase1(h).wait_send()
        phase2(h).wait_send()
        phase3(h).wait_send()
        return carry

    lax.fori_loop(0, heads, drain, 0)
    for p in range(3):
        id_phase(p).wait_send()


def body(sizes, queries, key_vectors, value_vectors, write_gate, ridge_term, segment_ids):
    tokens, width = queries.shape
    heads = ridge_term.shape[0]
    blocks = tokens // STRETCH
    vmem = pl.BlockSpec(memory_space=pltpu.VMEM)
    far = pl.BlockSpec(memory_space=pl.ANY)
    smem = pl.BlockSpec(memory_space=pltpu.SMEM)
    state = pltpu.VMEM((heads, 256, 128), F32)
    return pl.pallas_call(
        functools.partial(kernel, sizes),
        out_shape=jax.ShapeDtypeStruct((tokens, width), BF16),
        in_specs=[far, far, far, far, smem, far],
        out_specs=vmem,
        scratch_shapes=[
            pltpu.VMEM((tokens, width), BF16),
            pltpu.VMEM((tokens, width), BF16),
            pltpu.VMEM((tokens, width), BF16),
            pltpu.VMEM((heads, tokens), F32),
            pltpu.VMEM((blocks, STRETCH), jnp.int32),
            pltpu.SemaphoreType.DMA((5,)),
            pltpu.VMEM((blocks, STRETCH, STRETCH), F32),
            pltpu.VMEM((blocks, STRETCH, STRETCH), F32),
            pltpu.VMEM((blocks, STRETCH, STRETCH), BF16),
            pltpu.VMEM((heads, blocks, 128, STRETCH), BF16),
            pltpu.VMEM((heads, blocks, 1, STRETCH), F32),
            pltpu.VMEM((heads, blocks, 1, STRETCH), F32),
            pltpu.VMEM((heads, blocks - 1, 256, 128), F32),
            state, state, state, state, state, state,
            pltpu.VMEM((3, 8, 128), F32),
            pltpu.VMEM((3, 8, 128), F32),
        ] + [pltpu.SemaphoreType.DMA((heads,))] * 6 + [pltpu.SemaphoreType.DMA((3,))] * 2,
        compiler_params=pltpu.CompilerParams(
            collective_id=0, has_side_effects=True, vmem_limit_bytes=60 * 1024 * 1024
        ),
        cost_estimate=pl.CostEstimate(
            flops=6_000_000_000, bytes_accessed=6_000_000, transcendentals=0
        ),
    )(
        queries, key_vectors, value_vectors, write_gate, ridge_term,
        segment_ids.reshape(blocks, STRETCH),
    )


def solution(mesh):
    sizes = (mesh.shape["outer"], mesh.shape["inner"])
    return jax.shard_map(
        functools.partial(body, sizes),
        mesh=mesh,
        in_specs=(
            P(("outer", "inner"), None),
            P(("outer", "inner"), None),
            P(("outer", "inner"), None),
            P(None, ("outer", "inner")),
            P(),
            P(("outer", "inner")),
        ),
        out_specs=P(("outer", "inner"), None),
        check_vma=False,
    )
```

```python
import functools

import jax
import jax.numpy as jnp
from jax import lax
from jax.experimental import pallas as pl
from jax.experimental.pallas import tpu as pltpu
from jax.sharding import PartitionSpec as P

STRETCH = 128
ITERS = 4
PAIR = 2
MESH = pl.DeviceIdType.MESH
F32 = jnp.float32
BF16 = jnp.bfloat16


def split(x):
    hi = x.astype(BF16)
    return hi, (x - hi.astype(F32)).astype(BF16)


def mm(a, b):
    return jnp.dot(a, b, preferred_element_type=F32)


def same(a, b):
    return (a == b).astype(F32)


def kernel(
    sizes, q_far, k_far, v_far, gate_far, ridge_ref, seg_far, o_ref,
    q_ref, k_ref, v_ref, gate_ref, seg_ref, load_sem,
    causal, causal_t, keep, kt_buf, gram_row, memory_row, part,
    local, got1, pair, got2, suffix, got3, id_out, id_in,
    send1, recv1, send2, recv2, send3, recv3, id_send, id_recv,
):
    loads = [
        pltpu.make_async_copy(far, near, load_sem.at[i])
        for i, (far, near) in enumerate((
            (seg_far, seg_ref), (k_far, k_ref), (gate_far, gate_ref),
            (v_far, v_ref), (q_far, q_ref),
        ))
    ]
    for load in loads:
        load.start()
    outer, inner = sizes
    devices = outer * inner
    heads = gate_ref.shape[0]
    blocks = q_ref.shape[0] // STRETCH
    me = lax.axis_index("outer") * inner + lax.axis_index("inner")
    spot = me % 4
    odd_i, top_i = spot % 2, spot // 2

    def place(index):
        return (index // inner, index % inner)

    across1 = place(me + 1 - 2 * odd_i)
    across2 = place(me + 2 - 4 * top_i)
    after = place((me + 4) % devices)
    before = place((me + devices - 4) % devices)

    barrier = pltpu.get_barrier_semaphore()
    for target in (across1, across2, before):
        pl.semaphore_signal(barrier, inc=1, device_id=target, device_id_type=MESH)
    pl.semaphore_wait(barrier, 3)

    def exchange(src, dst, sender, receiver, target):
        return pltpu.make_async_remote_copy(
            src_ref=src, dst_ref=dst, send_sem=sender, recv_sem=receiver,
            device_id=target, device_id_type=MESH,
        )

    def phase1(h):
        return exchange(local.at[h], got1.at[h], send1.at[h], recv1.at[h], across1)

    def phase2(h):
        return exchange(pair.at[h], got2.at[h], send2.at[h], recv2.at[h], across2)

    def phase3(h):
        return exchange(suffix.at[h], got3.at[h], send3.at[h], recv3.at[h], after)

    def id_phase(p):
        target = (across1, across2, after)[p]
        return exchange(id_out.at[p], id_in.at[p], id_send.at[p], id_recv.at[p], target)

    loads[0].wait()
    seg = seg_ref[...].astype(F32)
    first = seg[0:1, 0:1]
    rows = [seg[b:b + 1, :] for b in range(blocks)]
    last = [seg[b:b + 1, STRETCH - 1:STRETCH] for b in range(blocks)]

    id_out[0] = jnp.broadcast_to(last[-1], (8, 128))
    id_phase(0).start()

    odd, top = odd_i.astype(F32), top_i.astype(F32)
    for b in range(blocks):
        grid_rows = jnp.broadcast_to(rows[b], (STRETCH, STRETCH))
        grid_cols = grid_rows.T
        down = lax.broadcasted_iota(jnp.int32, (STRETCH, STRETCH), 0)
        over = lax.broadcasted_iota(jnp.int32, (STRETCH, STRETCH), 1)
        causal[b] = jnp.where(over <= down, same(grid_rows, grid_cols), 0.0)
        causal_t[b] = causal[b].T
        keep[b] = same(grid_cols, first if b == 0 else last[b - 1]).astype(BF16)

    tails = [same(rows[b], last[b]) for b in range(blocks)]

    def columns(h):
        return pl.ds(pl.multiple_of(h * 128, 128), 128)

    def span(b):
        return slice(b * STRETCH, (b + 1) * STRETCH)

    def gather_local(h, carry):
        total = jnp.zeros((256, 128), F32)
        for b in range(blocks):
            keys = k_ref[span(b), columns(h)]
            values = v_ref[span(b), columns(h)]
            wide = keys.astype(F32).T
            kt_buf[h, b] = wide.astype(BF16)
            scale = lax.rsqrt(jnp.sum(wide * wide, axis=0, keepdims=True) + 1e-06)
            w1 = memory_row[h, b] * scale
            w2 = w1 * scale
            memory_row[h, b] = w1
            gram_row[h, b] = w2
            ghi, glo = split(wide * (w2 * tails[b]))
            mhi, mlo = split(wide * (w1 * tails[b]))
            gram = mm(jnp.concatenate([ghi, glo], 1), jnp.concatenate([keys, keys], 0))
            memory = mm(jnp.concatenate([mhi, mlo], 1), jnp.concatenate([values, values], 0))
            both = jnp.concatenate([gram, memory], 0)
            if b < blocks - 1:
                part[h, b] = both
            total = total + same(last[b], last[-1]) * both
        local[h] = total
        phase1(h).start()
        return carry

    for load in loads[1:4]:
        load.wait()
    for h in range(heads):
        for b in range(blocks):
            memory_row[h, b] = gate_ref[h:h + 1, span(b)]
    lax.fori_loop(0, 3, gather_local, 0)
    id_phase(0).wait_recv()
    other_last = id_in[0][0:1, 0:1]
    equal = same(last[-1], other_last)
    pair_local = odd + (1.0 - odd) * equal
    pair_got = (1.0 - odd) + odd * equal
    pair_id = odd * last[-1] + (1.0 - odd) * other_last
    id_out[1] = jnp.broadcast_to(pair_id, (8, 128))
    id_phase(1).start()
    lax.fori_loop(3, 5, gather_local, 0)
    id_phase(1).wait_recv()
    far_id = id_in[1][0:1, 0:1]
    base = top + (1.0 - top) * same(pair_id, far_id)
    suffix_local = base * (odd + (1.0 - odd) * pair_local)
    suffix_got = base * (1.0 - odd) * pair_got
    id_out[2] = jnp.broadcast_to(top * pair_id + (1.0 - top) * far_id, (8, 128))
    id_phase(2).start()

    def solve(base):
        items = [(base + i, b) for i in range(PAIR) for b in range(blocks)]
        every = range(len(items))
        mems, firsts, lows, seconds, weights, held, ridges = [], [], [], [], [], [], []
        xs, rs, ds, sqs = [], [], [], []
        state = None
        for h, b in items:
            if b == 0:
                state = in1 * got1[h] + in2 * got2[h] + in3 * got3[h]
            else:
                previous = first if b == 1 else last[b - 2]
                state = part[h, b - 1] + same(last[b - 1], previous) * state
            hi, lo = split(state)
            k = k_ref[span(b), columns(h)]
            v = v_ref[span(b), columns(h)]
            kt = kt_buf[h, b]
            firsts.append(jnp.concatenate([k, hi[:128]], 0))
            lows.append(lo[:128])
            seconds.append(jnp.concatenate([kt, kt], 1))
            mems.append(jnp.concatenate([v, v, hi[128:], hi[128:], lo[128:]], 0))
            column = jnp.broadcast_to(gram_row[h, b], (8, STRETCH)).T[:, 0:1]
            weights.append(causal_t[b] * column)
            held.append(same(rows[b], first if b == 0 else last[b - 1]))
            ridges.append(ridge_ref[h])
            q = q_ref[span(b), columns(h)].astype(F32).T
            q = q * lax.rsqrt(jnp.sum(q * q, axis=0, keepdims=True) + 1e-06)
            rs.append(q)
            ds.append(q)
            sqs.append(jnp.sum(q * q, axis=0, keepdims=True))

        for sweep in range(ITERS - 1):
            cuts = [split(ds[c]) for c in every]
            raised = [
                mm(jnp.concatenate([firsts[c]] * 2, 1), jnp.concatenate(cuts[c], 0)) for c in every
            ]
            lowered = [mm(lows[c], cuts[c][0]) for c in every]
            scores = [split(raised[c][:128] * weights[c]) for c in every]
            inside = [mm(seconds[c], jnp.concatenate(scores[c], 0)) for c in every]
            for c in every:
                d = ds[c]
                image = inside[c] + held[c] * (raised[c][128:] + lowered[c]) + ridges[c] * d
                size = sqs[c] / jnp.sum(d * image, axis=0, keepdims=True)
                if sweep == 0:
                    xs.append(size * d)
                else:
                    xs[c] = xs[c] + size * d
                rs[c] = rs[c] - size * image
                fresh = jnp.sum(rs[c] * rs[c], axis=0, keepdims=True)
                ds[c] = rs[c] + fresh / sqs[c] * d
                sqs[c] = fresh
        raised = [mm(firsts[c], ds[c].astype(BF16)) for c in every]
        for c in every:
            d, scores = ds[c], raised[c][:128]
            form = scores * scores * weights[c] + d * (held[c] * raised[c][128:] + ridges[c] * d)
            xs[c] = xs[c] + sqs[c] / jnp.sum(form, axis=0, keepdims=True) * d

        cuts = [split(xs[c].T) for c in every]
        scores = []
        for c, (h, b) in enumerate(items):
            kt = kt_buf[h, b]
            scores.append(mm(jnp.concatenate(cuts[c], 1), jnp.concatenate([kt, kt], 0)))
        for c, (h, b) in enumerate(items):
            shi, slo = split(scores[c] * (causal[b] * memory_row[h, b]))
            hi, lo = cuts[c]
            mask = keep[b]
            khi, klo = hi * mask, lo * mask
            out = mm(jnp.concatenate([shi, slo, khi, klo, khi], 1), mems[c])
            o_ref[span(b), columns(h)] = out.astype(BF16)

    def relay1(h):
        phase1(h).wait_recv()
        pair[h] = pair_local * local[h] + pair_got * got1[h]
        phase2(h).start()

    def relay2(h):
        phase2(h).wait_recv()
        suffix[h] = (1.0 - top) * got2[h] + suffix_local * local[h] + suffix_got * got1[h]
        phase3(h).start()

    relay1(0)
    lax.fori_loop(5, 8, gather_local, 0)
    relay1(1)
    lax.fori_loop(8, heads, gather_local, 0)
    relay1(2)
    loads[4].wait()
    id_phase(2).wait_recv()
    in1 = odd * same(other_last, first)
    in2 = top * same(far_id, first)
    in3 = same(id_in[2][0:1, 0:1], first)
    relay1(3)
    relay2(0)
    relay2(1)
    groups = heads // PAIR

    def stage(t, carry):
        @pl.when(t < groups - 2)
        def _():
            for i in range(PAIR):
                relay1(PAIR * (t + 2) + i)

        @pl.when(t < groups - 1)
        def _():
            for i in range(PAIR):
                relay2(PAIR * (t + 1) + i)

        for i in range(PAIR):
            phase3(PAIR * t + i).wait_recv()
        solve(PAIR * t)
        return carry

    lax.fori_loop(0, groups, stage, 0)

    def drain(h, carry):
        phase1(h).wait_send()
        phase2(h).wait_send()
        phase3(h).wait_send()
        return carry

    lax.fori_loop(0, heads, drain, 0)
    for p in range(3):
        id_phase(p).wait_send()


def body(sizes, queries, key_vectors, value_vectors, write_gate, ridge_term, segment_ids):
    tokens, width = queries.shape
    heads = ridge_term.shape[0]
    blocks = tokens // STRETCH
    vmem = pl.BlockSpec(memory_space=pltpu.VMEM)
    far = pl.BlockSpec(memory_space=pl.ANY)
    smem = pl.BlockSpec(memory_space=pltpu.SMEM)
    state = pltpu.VMEM((heads, 256, 128), F32)
    return pl.pallas_call(
        functools.partial(kernel, sizes),
        out_shape=jax.ShapeDtypeStruct((tokens, width), BF16),
        in_specs=[far, far, far, far, smem, far],
        out_specs=vmem,
        scratch_shapes=[
            pltpu.VMEM((tokens, width), BF16),
            pltpu.VMEM((tokens, width), BF16),
            pltpu.VMEM((tokens, width), BF16),
            pltpu.VMEM((heads, tokens), F32),
            pltpu.VMEM((blocks, STRETCH), jnp.int32),
            pltpu.SemaphoreType.DMA((5,)),
            pltpu.VMEM((blocks, STRETCH, STRETCH), F32),
            pltpu.VMEM((blocks, STRETCH, STRETCH), F32),
            pltpu.VMEM((blocks, STRETCH, STRETCH), BF16),
            pltpu.VMEM((heads, blocks, 128, STRETCH), BF16),
            pltpu.VMEM((heads, blocks, 1, STRETCH), F32),
            pltpu.VMEM((heads, blocks, 1, STRETCH), F32),
            pltpu.VMEM((heads, blocks - 1, 256, 128), F32),
            state, state, state, state, state, state,
            pltpu.VMEM((3, 8, 128), F32),
            pltpu.VMEM((3, 8, 128), F32),
        ] + [pltpu.SemaphoreType.DMA((heads,))] * 6 + [pltpu.SemaphoreType.DMA((3,))] * 2,
        compiler_params=pltpu.CompilerParams(
            collective_id=0, has_side_effects=True, vmem_limit_bytes=60 * 1024 * 1024
        ),
        cost_estimate=pl.CostEstimate(
            flops=6_000_000_000, bytes_accessed=6_000_000, transcendentals=0
        ),
    )(
        queries, key_vectors, value_vectors, write_gate, ridge_term,
        segment_ids.reshape(blocks, STRETCH),
    )


def solution(mesh):
    sizes = (mesh.shape["outer"], mesh.shape["inner"])
    return jax.shard_map(
        functools.partial(body, sizes),
        mesh=mesh,
        in_specs=(
            P(("outer", "inner"), None),
            P(("outer", "inner"), None),
            P(("outer", "inner"), None),
            P(None, ("outer", "inner")),
            P(),
            P(("outer", "inner")),
        ),
        out_specs=P(("outer", "inner"), None),
        check_vma=False,
    )
```

```python
import functools

import jax
import jax.numpy as jnp
from jax import lax
from jax.experimental import pallas as pl
from jax.experimental.pallas import tpu as pltpu
from jax.sharding import PartitionSpec as P

STRETCH = 128
ITERS = 4
PAIR = 2
MESH = pl.DeviceIdType.MESH
F32 = jnp.float32
BF16 = jnp.bfloat16


def split(x):
    hi = x.astype(BF16)
    return hi, (x - hi.astype(F32)).astype(BF16)


def mm(a, b):
    return jnp.dot(a, b, preferred_element_type=F32)


def same(a, b):
    return (a == b).astype(F32)


def kernel(
    sizes, q_far, k_far, v_far, gate_far, ridge_ref, seg_far, o_ref,
    q_ref, k_ref, v_ref, gate_ref, seg_ref, load_sem,
    causal, causal_t, keep, kt_buf, gram_row, memory_row, part,
    local, got1, pair, got2, suffix, got3, id_out, id_in,
    send1, recv1, send2, recv2, send3, recv3, id_send, id_recv,
):
    loads = [
        pltpu.make_async_copy(far, near, load_sem.at[i])
        for i, (far, near) in enumerate((
            (seg_far, seg_ref), (k_far, k_ref), (gate_far, gate_ref),
            (v_far, v_ref), (q_far, q_ref),
        ))
    ]
    for load in loads:
        load.start()
    outer, inner = sizes
    devices = outer * inner
    heads = gate_ref.shape[0]
    blocks = q_ref.shape[0] // STRETCH
    me = lax.axis_index("outer") * inner + lax.axis_index("inner")
    spot = me % 4
    odd_i, top_i = spot % 2, spot // 2

    def place(index):
        return (index // inner, index % inner)

    across1 = place(me + 1 - 2 * odd_i)
    across2 = place(me + 2 - 4 * top_i)
    after = place((me + 4) % devices)
    before = place((me + devices - 4) % devices)

    barrier = pltpu.get_barrier_semaphore()
    for target in (across1, across2, before):
        pl.semaphore_signal(barrier, inc=1, device_id=target, device_id_type=MESH)
    pl.semaphore_wait(barrier, 3)

    def exchange(src, dst, sender, receiver, target):
        return pltpu.make_async_remote_copy(
            src_ref=src, dst_ref=dst, send_sem=sender, recv_sem=receiver,
            device_id=target, device_id_type=MESH,
        )

    def phase1(h):
        return exchange(local.at[h], got1.at[h], send1.at[h], recv1.at[h], across1)

    def phase2(h):
        return exchange(pair.at[h], got2.at[h], send2.at[h], recv2.at[h], across2)

    def phase3(h):
        return exchange(suffix.at[h], got3.at[h], send3.at[h], recv3.at[h], after)

    def id_phase(p):
        target = (across1, across2, after)[p]
        return exchange(id_out.at[p], id_in.at[p], id_send.at[p], id_recv.at[p], target)

    loads[0].wait()
    seg = seg_ref[...].astype(F32)
    first = seg[0:1, 0:1]
    rows = [seg[b:b + 1, :] for b in range(blocks)]
    last = [seg[b:b + 1, STRETCH - 1:STRETCH] for b in range(blocks)]

    id_out[0] = jnp.broadcast_to(last[-1], (8, 128))
    id_phase(0).start()

    odd, top = odd_i.astype(F32), top_i.astype(F32)
    for b in range(blocks):
        grid_rows = jnp.broadcast_to(rows[b], (STRETCH, STRETCH))
        grid_cols = grid_rows.T
        down = lax.broadcasted_iota(jnp.int32, (STRETCH, STRETCH), 0)
        over = lax.broadcasted_iota(jnp.int32, (STRETCH, STRETCH), 1)
        causal[b] = jnp.where(over <= down, same(grid_rows, grid_cols), 0.0)
        causal_t[b] = causal[b].T
        keep[b] = same(grid_cols, first if b == 0 else last[b - 1]).astype(BF16)

    tails = [same(rows[b], last[b]) for b in range(blocks)]

    def columns(h):
        return pl.ds(pl.multiple_of(h * 128, 128), 128)

    def span(b):
        return slice(b * STRETCH, (b + 1) * STRETCH)

    half_down = lax.broadcasted_iota(jnp.int32, (64, 128), 0)
    half_over = lax.broadcasted_iota(jnp.int32, (64, 128), 1)

    def square(packed):
        flat = packed[128:192]
        turned = jnp.concatenate([flat, jnp.zeros_like(flat)], 0).T
        upper = jnp.where(half_down <= half_over, flat, turned[0:64])
        low = jnp.where(half_down > half_over, flat, turned[0:64])
        low = jnp.where(half_down == half_over, packed[192:193], low)
        lower = jnp.where(half_over < 64, turned[64:128], pltpu.roll(low, 64, 1))
        return jnp.concatenate([upper, lower, packed[0:128]], 0)

    def gather_local(h, carry):
        total = jnp.zeros((256, 128), F32)
        for b in range(blocks):
            keys = k_ref[span(b), columns(h)]
            values = v_ref[span(b), columns(h)]
            wide = keys.astype(F32).T
            kt_buf[h, b] = wide.astype(BF16)
            scale = lax.rsqrt(jnp.sum(wide * wide, axis=0, keepdims=True) + 1e-06)
            w1 = memory_row[h, b] * scale
            w2 = w1 * scale
            memory_row[h, b] = w1
            gram_row[h, b] = w2
            ghi, glo = split(wide * (w2 * tails[b]))
            mhi, mlo = split(wide * (w1 * tails[b]))
            gram = mm(jnp.concatenate([ghi, glo], 1), jnp.concatenate([keys, keys], 0))
            memory = mm(jnp.concatenate([mhi, mlo], 1), jnp.concatenate([values, values], 0))
            both = jnp.concatenate([gram, memory], 0)
            if b < blocks - 1:
                part[h, b] = both
            total = total + same(last[b], last[-1]) * both
        low = pltpu.roll(total[64:128], 64, 1)
        local[h, 0:128] = total[128:256]
        local[h, 128:192] = jnp.where(half_down > half_over, low, total[0:64])
        corner = jnp.sum(jnp.where(half_down == half_over, low, 0.0), axis=0, keepdims=True)
        local[h, 192:200] = jnp.broadcast_to(corner, (8, 128))
        phase1(h).start()
        return carry

    for load in loads[1:4]:
        load.wait()
    for h in range(heads):
        for b in range(blocks):
            memory_row[h, b] = gate_ref[h:h + 1, span(b)]
    lax.fori_loop(0, 3, gather_local, 0)
    id_phase(0).wait_recv()
    other_last = id_in[0][0:1, 0:1]
    equal = same(last[-1], other_last)
    pair_local = odd + (1.0 - odd) * equal
    pair_got = (1.0 - odd) + odd * equal
    pair_id = odd * last[-1] + (1.0 - odd) * other_last
    id_out[1] = jnp.broadcast_to(pair_id, (8, 128))
    id_phase(1).start()
    lax.fori_loop(3, 5, gather_local, 0)
    id_phase(1).wait_recv()
    far_id = id_in[1][0:1, 0:1]
    base = top + (1.0 - top) * same(pair_id, far_id)
    suffix_local = base * (odd + (1.0 - odd) * pair_local)
    suffix_got = base * (1.0 - odd) * pair_got
    id_out[2] = jnp.broadcast_to(top * pair_id + (1.0 - top) * far_id, (8, 128))
    id_phase(2).start()

    def solve(base):
        items = [(base + i, b) for i in range(PAIR) for b in range(blocks)]
        every = range(len(items))
        mems, firsts, lows, seconds, weights, held, ridges = [], [], [], [], [], [], []
        xs, rs, ds, sqs = [], [], [], []
        state = None
        for h, b in items:
            if b == 0:
                state = square(in1 * got1[h] + in2 * got2[h] + in3 * got3[h])
            else:
                previous = first if b == 1 else last[b - 2]
                state = part[h, b - 1] + same(last[b - 1], previous) * state
            hi, lo = split(state)
            k = k_ref[span(b), columns(h)]
            v = v_ref[span(b), columns(h)]
            kt = kt_buf[h, b]
            firsts.append(jnp.concatenate([k, hi[:128]], 0))
            lows.append(lo[:128])
            seconds.append(jnp.concatenate([kt, kt], 1))
            mems.append(jnp.concatenate([v, v, hi[128:], hi[128:], lo[128:]], 0))
            column = jnp.broadcast_to(gram_row[h, b], (8, STRETCH)).T[:, 0:1]
            weights.append(causal_t[b] * column)
            held.append(same(rows[b], first if b == 0 else last[b - 1]))
            ridges.append(ridge_ref[h])
            q = q_ref[span(b), columns(h)].astype(F32).T
            q = q * lax.rsqrt(jnp.sum(q * q, axis=0, keepdims=True) + 1e-06)
            rs.append(q)
            ds.append(q)
            sqs.append(jnp.sum(q * q, axis=0, keepdims=True))

        for sweep in range(ITERS - 1):
            cuts = [split(ds[c]) for c in every]
            raised = [
                mm(jnp.concatenate([firsts[c]] * 2, 1), jnp.concatenate(cuts[c], 0)) for c in every
            ]
            lowered = [mm(lows[c], cuts[c][0]) for c in every]
            scores = [split(raised[c][:128] * weights[c]) for c in every]
            inside = [mm(seconds[c], jnp.concatenate(scores[c], 0)) for c in every]
            for c in every:
                d = ds[c]
                image = inside[c] + held[c] * (raised[c][128:] + lowered[c]) + ridges[c] * d
                size = sqs[c] / jnp.sum(d * image, axis=0, keepdims=True)
                if sweep == 0:
                    xs.append(size * d)
                else:
                    xs[c] = xs[c] + size * d
                rs[c] = rs[c] - size * image
                fresh = jnp.sum(rs[c] * rs[c], axis=0, keepdims=True)
                ds[c] = rs[c] + fresh / sqs[c] * d
                sqs[c] = fresh
        raised = [mm(firsts[c], ds[c].astype(BF16)) for c in every]
        for c in every:
            d, scores = ds[c], raised[c][:128]
            form = scores * scores * weights[c] + d * (held[c] * raised[c][128:] + ridges[c] * d)
            xs[c] = xs[c] + sqs[c] / jnp.sum(form, axis=0, keepdims=True) * d

        cuts = [split(xs[c].T) for c in every]
        scores = []
        for c, (h, b) in enumerate(items):
            kt = kt_buf[h, b]
            scores.append(mm(jnp.concatenate(cuts[c], 1), jnp.concatenate([kt, kt], 0)))
        for c, (h, b) in enumerate(items):
            shi, slo = split(scores[c] * (causal[b] * memory_row[h, b]))
            hi, lo = cuts[c]
            mask = keep[b]
            khi, klo = hi * mask, lo * mask
            out = mm(jnp.concatenate([shi, slo, khi, klo, khi], 1), mems[c])
            o_ref[span(b), columns(h)] = out.astype(BF16)

    def relay1(h):
        phase1(h).wait_recv()
        pair[h] = pair_local * local[h] + pair_got * got1[h]
        phase2(h).start()

    def relay2(h):
        phase2(h).wait_recv()
        suffix[h] = (1.0 - top) * got2[h] + suffix_local * local[h] + suffix_got * got1[h]
        phase3(h).start()

    relay1(0)
    lax.fori_loop(5, 8, gather_local, 0)
    relay1(1)
    lax.fori_loop(8, heads, gather_local, 0)
    relay1(2)
    loads[4].wait()
    id_phase(2).wait_recv()
    in1 = odd * same(other_last, first)
    in2 = top * same(far_id, first)
    in3 = same(id_in[2][0:1, 0:1], first)
    relay1(3)
    relay2(0)
    relay2(1)
    groups = heads // PAIR

    def stage(t, carry):
        @pl.when(t < groups - 2)
        def _():
            for i in range(PAIR):
                relay1(PAIR * (t + 2) + i)

        @pl.when(t < groups - 1)
        def _():
            for i in range(PAIR):
                relay2(PAIR * (t + 1) + i)

        for i in range(PAIR):
            phase3(PAIR * t + i).wait_recv()
        solve(PAIR * t)
        return carry

    lax.fori_loop(0, groups, stage, 0)

    def drain(h, carry):
        phase1(h).wait_send()
        phase2(h).wait_send()
        phase3(h).wait_send()
        return carry

    lax.fori_loop(0, heads, drain, 0)
    for p in range(3):
        id_phase(p).wait_send()


def body(sizes, queries, key_vectors, value_vectors, write_gate, ridge_term, segment_ids):
    tokens, width = queries.shape
    heads = ridge_term.shape[0]
    blocks = tokens // STRETCH
    vmem = pl.BlockSpec(memory_space=pltpu.VMEM)
    far = pl.BlockSpec(memory_space=pl.ANY)
    smem = pl.BlockSpec(memory_space=pltpu.SMEM)
    state = pltpu.VMEM((heads, 200, 128), F32)
    return pl.pallas_call(
        functools.partial(kernel, sizes),
        out_shape=jax.ShapeDtypeStruct((tokens, width), BF16),
        in_specs=[far, far, far, far, smem, far],
        out_specs=vmem,
        scratch_shapes=[
            pltpu.VMEM((tokens, width), BF16),
            pltpu.VMEM((tokens, width), BF16),
            pltpu.VMEM((tokens, width), BF16),
            pltpu.VMEM((heads, tokens), F32),
            pltpu.VMEM((blocks, STRETCH), jnp.int32),
            pltpu.SemaphoreType.DMA((5,)),
            pltpu.VMEM((blocks, STRETCH, STRETCH), F32),
            pltpu.VMEM((blocks, STRETCH, STRETCH), F32),
            pltpu.VMEM((blocks, STRETCH, STRETCH), BF16),
            pltpu.VMEM((heads, blocks, 128, STRETCH), BF16),
            pltpu.VMEM((heads, blocks, 1, STRETCH), F32),
            pltpu.VMEM((heads, blocks, 1, STRETCH), F32),
            pltpu.VMEM((heads, blocks - 1, 256, 128), F32),
            state, state, state, state, state, state,
            pltpu.VMEM((3, 8, 128), F32),
            pltpu.VMEM((3, 8, 128), F32),
        ] + [pltpu.SemaphoreType.DMA((heads,))] * 6 + [pltpu.SemaphoreType.DMA((3,))] * 2,
        compiler_params=pltpu.CompilerParams(
            collective_id=0, has_side_effects=True, vmem_limit_bytes=60 * 1024 * 1024
        ),
        cost_estimate=pl.CostEstimate(
            flops=6_000_000_000, bytes_accessed=6_000_000, transcendentals=0
        ),
    )(
        queries, key_vectors, value_vectors, write_gate, ridge_term,
        segment_ids.reshape(blocks, STRETCH),
    )


def solution(mesh):
    sizes = (mesh.shape["outer"], mesh.shape["inner"])
    return jax.shard_map(
        functools.partial(body, sizes),
        mesh=mesh,
        in_specs=(
            P(("outer", "inner"), None),
            P(("outer", "inner"), None),
            P(("outer", "inner"), None),
            P(None, ("outer", "inner")),
            P(),
            P(("outer", "inner")),
        ),
        out_specs=P(("outer", "inner"), None),
        check_vma=False,
    )
```

```python
import functools

import jax
import jax.numpy as jnp
from jax import lax
from jax.experimental import pallas as pl
from jax.experimental.pallas import tpu as pltpu
from jax.sharding import PartitionSpec as P

STRETCH = 128
ITERS = 4
PAIR = 2
MESH = pl.DeviceIdType.MESH
F32 = jnp.float32
BF16 = jnp.bfloat16


def split(x):
    hi = x.astype(BF16)
    return hi, (x - hi.astype(F32)).astype(BF16)


def mm(a, b):
    return jnp.dot(a, b, preferred_element_type=F32)


def same(a, b):
    return (a == b).astype(F32)


def kernel(
    sizes, q_far, k_far, v_far, gate_far, ridge_ref, seg_far, o_ref,
    q_ref, k_ref, v_ref, gate_ref, seg_ref, load_sem,
    causal, causal_t, keep, kt_buf, gram_row, memory_row, part,
    local, got1, pair, got2, suffix, got3, id_out, id_in,
    send1, recv1, send2, recv2, send3, recv3, id_send, id_recv,
):
    loads = [
        pltpu.make_async_copy(far, near, load_sem.at[i])
        for i, (far, near) in enumerate((
            (seg_far, seg_ref), (k_far, k_ref), (gate_far, gate_ref),
            (v_far, v_ref), (q_far, q_ref),
        ))
    ]
    for load in loads:
        load.start()
    outer, inner = sizes
    devices = outer * inner
    heads = gate_ref.shape[0]
    blocks = q_ref.shape[0] // STRETCH
    me = lax.axis_index("outer") * inner + lax.axis_index("inner")
    spot = me % 4
    odd_i, top_i = spot % 2, spot // 2

    def place(index):
        return (index // inner, index % inner)

    across1 = place(me + 1 - 2 * odd_i)
    across2 = place(me + 2 - 4 * top_i)
    after = place((me + 4) % devices)
    before = place((me + devices - 4) % devices)

    barrier = pltpu.get_barrier_semaphore()
    for target in (across1, across2, before):
        pl.semaphore_signal(barrier, inc=1, device_id=target, device_id_type=MESH)
    pl.semaphore_wait(barrier, 3)

    def exchange(src, dst, sender, receiver, target):
        return pltpu.make_async_remote_copy(
            src_ref=src, dst_ref=dst, send_sem=sender, recv_sem=receiver,
            device_id=target, device_id_type=MESH,
        )

    def phase1(h):
        return exchange(local.at[h], got1.at[h], send1.at[h], recv1.at[h], across1)

    def phase2(h):
        return exchange(pair.at[h], got2.at[h], send2.at[h], recv2.at[h], across2)

    def phase3(h):
        return exchange(suffix.at[h], got3.at[h], send3.at[h], recv3.at[h], after)

    def id_phase(p):
        target = (across1, across2, after)[p]
        return exchange(id_out.at[p], id_in.at[p], id_send.at[p], id_recv.at[p], target)

    loads[0].wait()
    seg = seg_ref[...].astype(F32)
    first = seg[0:1, 0:1]
    rows = [seg[b:b + 1, :] for b in range(blocks)]
    last = [seg[b:b + 1, STRETCH - 1:STRETCH] for b in range(blocks)]

    id_out[0] = jnp.broadcast_to(last[-1], (8, 128))
    id_phase(0).start()

    odd, top = odd_i.astype(F32), top_i.astype(F32)
    for b in range(blocks):
        grid_rows = jnp.broadcast_to(rows[b], (STRETCH, STRETCH))
        grid_cols = grid_rows.T
        down = lax.broadcasted_iota(jnp.int32, (STRETCH, STRETCH), 0)
        over = lax.broadcasted_iota(jnp.int32, (STRETCH, STRETCH), 1)
        causal[b] = jnp.where(over <= down, same(grid_rows, grid_cols), 0.0)
        causal_t[b] = causal[b].T
        keep[b] = same(grid_cols, first if b == 0 else last[b - 1]).astype(BF16)

    tails = [same(rows[b], last[b]) for b in range(blocks)]

    def columns(h):
        return pl.ds(pl.multiple_of(h * 128, 128), 128)

    def span(b):
        return slice(b * STRETCH, (b + 1) * STRETCH)

    half_down = lax.broadcasted_iota(jnp.int32, (64, 128), 0)
    half_over = lax.broadcasted_iota(jnp.int32, (64, 128), 1)

    def square(packed):
        flat = packed[128:192]
        turned = jnp.concatenate([flat, jnp.zeros_like(flat)], 0).T
        upper = jnp.where(half_down <= half_over, flat, turned[0:64])
        low = jnp.where(half_down > half_over, flat, turned[0:64])
        low = jnp.where(half_down == half_over, packed[192:193], low)
        lower = jnp.where(half_over < 64, turned[64:128], pltpu.roll(low, 64, 1))
        return jnp.concatenate([upper, lower, packed[0:128]], 0)

    def gather_local(h, carry):
        total = jnp.zeros((256, 128), F32)
        for b in range(blocks):
            keys = k_ref[span(b), columns(h)]
            values = v_ref[span(b), columns(h)]
            wide = keys.astype(F32).T
            kt_buf[h, b] = wide.astype(BF16)
            scale = lax.rsqrt(jnp.sum(wide * wide, axis=0, keepdims=True) + 1e-06)
            w1 = memory_row[h, b] * scale
            w2 = w1 * scale
            memory_row[h, b] = w1
            gram_row[h, b] = w2
            ghi, glo = split(wide * (w2 * tails[b]))
            mhi, mlo = split(wide * (w1 * tails[b]))
            gram = mm(jnp.concatenate([ghi, glo], 1), jnp.concatenate([keys, keys], 0))
            memory = mm(jnp.concatenate([mhi, mlo], 1), jnp.concatenate([values, values], 0))
            both = jnp.concatenate([gram, memory], 0)
            if b < blocks - 1:
                part[h, b] = both
            total = total + same(last[b], last[-1]) * both
        low = pltpu.roll(total[64:128], 64, 1)
        local[h, 0:128] = total[128:256]
        local[h, 128:192] = jnp.where(half_down > half_over, low, total[0:64])
        corner = jnp.sum(jnp.where(half_down == half_over, low, 0.0), axis=0, keepdims=True)
        local[h, 192:200] = jnp.broadcast_to(corner, (8, 128))
        phase1(h).start()
        return carry

    for load in loads[1:4]:
        load.wait()
    for h in range(heads):
        for b in range(blocks):
            memory_row[h, b] = gate_ref[h:h + 1, span(b)]
    lax.fori_loop(0, 3, gather_local, 0)
    id_phase(0).wait_recv()
    other_last = id_in[0][0:1, 0:1]
    equal = same(last[-1], other_last)
    pair_local = odd + (1.0 - odd) * equal
    pair_got = (1.0 - odd) + odd * equal
    pair_id = odd * last[-1] + (1.0 - odd) * other_last
    id_out[1] = jnp.broadcast_to(pair_id, (8, 128))
    id_phase(1).start()
    lax.fori_loop(3, 5, gather_local, 0)
    id_phase(1).wait_recv()
    far_id = id_in[1][0:1, 0:1]
    base = top + (1.0 - top) * same(pair_id, far_id)
    suffix_local = base * (odd + (1.0 - odd) * pair_local)
    suffix_got = base * (1.0 - odd) * pair_got
    id_out[2] = jnp.broadcast_to(top * pair_id + (1.0 - top) * far_id, (8, 128))
    id_phase(2).start()

    def solve(t):
        items = [(PAIR * t + i, b) for i in range(PAIR) for b in range(blocks)]
        every = range(len(items))
        mems, firsts, lows, seconds, weights, held, ridges = [], [], [], [], [], [], []
        xs, rs, ds, sqs = [], [], [], []
        state = None
        for h, b in items:
            if b == 0:
                state = square(in1 * got1[h] + in2 * got2[h] + in3 * got3[h])
            else:
                previous = first if b == 1 else last[b - 2]
                state = part[h, b - 1] + same(last[b - 1], previous) * state
            hi, lo = split(state)
            k = k_ref[span(b), columns(h)]
            v = v_ref[span(b), columns(h)]
            kt = kt_buf[h, b]
            firsts.append(jnp.concatenate([k, hi[:128]], 0))
            lows.append(lo[:128])
            seconds.append(jnp.concatenate([kt, kt], 1))
            mems.append(jnp.concatenate([v, v, hi[128:], hi[128:], lo[128:]], 0))
            column = jnp.broadcast_to(gram_row[h, b], (8, STRETCH)).T[:, 0:1]
            weights.append(causal_t[b] * column)
            held.append(same(rows[b], first if b == 0 else last[b - 1]))
            ridges.append(ridge_ref[h])
            q = q_ref[span(b), columns(h)].astype(F32).T
            q = q * lax.rsqrt(jnp.sum(q * q, axis=0, keepdims=True) + 1e-06)
            rs.append(q)
            ds.append(q)
            sqs.append(jnp.sum(q * q, axis=0, keepdims=True))

        for sweep in range(ITERS - 1):
            cuts = [split(ds[c]) for c in every]
            raised = [
                mm(jnp.concatenate([firsts[c]] * 2, 1), jnp.concatenate(cuts[c], 0)) for c in every
            ]
            lowered = [mm(lows[c], cuts[c][0]) for c in every]
            scores = [split(raised[c][:128] * weights[c]) for c in every]
            inside = [mm(seconds[c], jnp.concatenate(scores[c], 0)) for c in every]
            for c in every:
                d = ds[c]
                image = inside[c] + held[c] * (raised[c][128:] + lowered[c]) + ridges[c] * d
                size = sqs[c] / jnp.sum(d * image, axis=0, keepdims=True)
                if sweep == 0:
                    xs.append(size * d)
                else:
                    xs[c] = xs[c] + size * d
                rs[c] = rs[c] - size * image
                fresh = jnp.sum(rs[c] * rs[c], axis=0, keepdims=True)
                ds[c] = rs[c] + fresh / sqs[c] * d
                sqs[c] = fresh
            if sweep == 0:
                @pl.when(t < groups - 2)
                def _():
                    for i in range(PAIR):
                        relay1(PAIR * (t + 2) + i)
            if sweep == 1:
                @pl.when(t < groups - 1)
                def _():
                    for i in range(PAIR):
                        relay2(PAIR * (t + 1) + i)
        raised = [mm(firsts[c], ds[c].astype(BF16)) for c in every]
        for c in every:
            d, scores = ds[c], raised[c][:128]
            form = scores * scores * weights[c] + d * (held[c] * raised[c][128:] + ridges[c] * d)
            xs[c] = xs[c] + sqs[c] / jnp.sum(form, axis=0, keepdims=True) * d

        cuts = [split(xs[c].T) for c in every]
        scores = []
        for c, (h, b) in enumerate(items):
            kt = kt_buf[h, b]
            scores.append(mm(jnp.concatenate(cuts[c], 1), jnp.concatenate([kt, kt], 0)))
        for c, (h, b) in enumerate(items):
            shi, slo = split(scores[c] * (causal[b] * memory_row[h, b]))
            hi, lo = cuts[c]
            mask = keep[b]
            khi, klo = hi * mask, lo * mask
            out = mm(jnp.concatenate([shi, slo, khi, klo, khi], 1), mems[c])
            o_ref[span(b), columns(h)] = out.astype(BF16)

    def relay1(h):
        phase1(h).wait_recv()
        pair[h] = pair_local * local[h] + pair_got * got1[h]
        phase2(h).start()

    def relay2(h):
        phase2(h).wait_recv()
        suffix[h] = (1.0 - top) * got2[h] + suffix_local * local[h] + suffix_got * got1[h]
        phase3(h).start()

    relay1(0)
    lax.fori_loop(5, 8, gather_local, 0)
    relay1(1)
    lax.fori_loop(8, heads, gather_local, 0)
    relay1(2)
    loads[4].wait()
    id_phase(2).wait_recv()
    in1 = odd * same(other_last, first)
    in2 = top * same(far_id, first)
    in3 = same(id_in[2][0:1, 0:1], first)
    relay2(0)
    relay2(1)
    relay1(3)
    groups = heads // PAIR

    def stage(t, carry):
        for i in range(PAIR):
            phase3(PAIR * t + i).wait_recv()
        solve(t)
        return carry

    lax.fori_loop(0, groups, stage, 0)

    def drain(h, carry):
        phase1(h).wait_send()
        phase2(h).wait_send()
        phase3(h).wait_send()
        return carry

    lax.fori_loop(0, heads, drain, 0)
    for p in range(3):
        id_phase(p).wait_send()


def body(sizes, queries, key_vectors, value_vectors, write_gate, ridge_term, segment_ids):
    tokens, width = queries.shape
    heads = ridge_term.shape[0]
    blocks = tokens // STRETCH
    vmem = pl.BlockSpec(memory_space=pltpu.VMEM)
    far = pl.BlockSpec(memory_space=pl.ANY)
    smem = pl.BlockSpec(memory_space=pltpu.SMEM)
    state = pltpu.VMEM((heads, 200, 128), F32)
    return pl.pallas_call(
        functools.partial(kernel, sizes),
        out_shape=jax.ShapeDtypeStruct((tokens, width), BF16),
        in_specs=[far, far, far, far, smem, far],
        out_specs=vmem,
        scratch_shapes=[
            pltpu.VMEM((tokens, width), BF16),
            pltpu.VMEM((tokens, width), BF16),
            pltpu.VMEM((tokens, width), BF16),
            pltpu.VMEM((heads, tokens), F32),
            pltpu.VMEM((blocks, STRETCH), jnp.int32),
            pltpu.SemaphoreType.DMA((5,)),
            pltpu.VMEM((blocks, STRETCH, STRETCH), F32),
            pltpu.VMEM((blocks, STRETCH, STRETCH), F32),
            pltpu.VMEM((blocks, STRETCH, STRETCH), BF16),
            pltpu.VMEM((heads, blocks, 128, STRETCH), BF16),
            pltpu.VMEM((heads, blocks, 1, STRETCH), F32),
            pltpu.VMEM((heads, blocks, 1, STRETCH), F32),
            pltpu.VMEM((heads, blocks - 1, 256, 128), F32),
            state, state, state, state, state, state,
            pltpu.VMEM((3, 8, 128), F32),
            pltpu.VMEM((3, 8, 128), F32),
        ] + [pltpu.SemaphoreType.DMA((heads,))] * 6 + [pltpu.SemaphoreType.DMA((3,))] * 2,
        compiler_params=pltpu.CompilerParams(
            collective_id=0, has_side_effects=True, vmem_limit_bytes=60 * 1024 * 1024
        ),
        cost_estimate=pl.CostEstimate(
            flops=6_000_000_000, bytes_accessed=6_000_000, transcendentals=0
        ),
    )(
        queries, key_vectors, value_vectors, write_gate, ridge_term,
        segment_ids.reshape(blocks, STRETCH),
    )


def solution(mesh):
    sizes = (mesh.shape["outer"], mesh.shape["inner"])
    return jax.shard_map(
        functools.partial(body, sizes),
        mesh=mesh,
        in_specs=(
            P(("outer", "inner"), None),
            P(("outer", "inner"), None),
            P(("outer", "inner"), None),
            P(None, ("outer", "inner")),
            P(),
            P(("outer", "inner")),
        ),
        out_specs=P(("outer", "inner"), None),
        check_vma=False,
    )
```

```python
import functools

import jax
import jax.numpy as jnp
from jax import lax
from jax.experimental import pallas as pl
from jax.experimental.pallas import tpu as pltpu
from jax.sharding import PartitionSpec as P

STRETCH = 128
ITERS = 4
PAIR = 2
MESH = pl.DeviceIdType.MESH
F32 = jnp.float32
BF16 = jnp.bfloat16


def split(x):
    hi = x.astype(BF16)
    return hi, (x - hi.astype(F32)).astype(BF16)


def mm(a, b):
    return jnp.dot(a, b, preferred_element_type=F32)


def same(a, b):
    return (a == b).astype(F32)


def kernel(
    sizes, q_far, k_far, v_far, gate_far, ridge_ref, seg_far, o_ref,
    q_ref, k_ref, v_ref, gate_ref, seg_ref, load_sem,
    causal, causal_t, keep, kt_buf, gram_row, memory_row, part,
    local, got1, pair, got2, suffix, got3, id_out, id_in,
    send1, recv1, send2, recv2, send3, recv3, id_send, id_recv,
):
    loads = [
        pltpu.make_async_copy(far, near, load_sem.at[i])
        for i, (far, near) in enumerate((
            (seg_far, seg_ref), (k_far, k_ref), (gate_far, gate_ref),
            (v_far, v_ref), (q_far, q_ref),
        ))
    ]
    for load in loads:
        load.start()
    outer, inner = sizes
    devices = outer * inner
    heads = gate_ref.shape[0]
    blocks = q_ref.shape[0] // STRETCH
    me = lax.axis_index("outer") * inner + lax.axis_index("inner")
    spot = me % 4
    odd_i, top_i = spot % 2, spot // 2

    def place(index):
        return (index // inner, index % inner)

    across1 = place(me + 1 - 2 * odd_i)
    across2 = place(me + 2 - 4 * top_i)
    after = place((me + 4) % devices)
    before = place((me + devices - 4) % devices)

    barrier = pltpu.get_barrier_semaphore()
    for target in (across1, across2, before):
        pl.semaphore_signal(barrier, inc=1, device_id=target, device_id_type=MESH)
    pl.semaphore_wait(barrier, 3)

    def exchange(src, dst, sender, receiver, target):
        return pltpu.make_async_remote_copy(
            src_ref=src, dst_ref=dst, send_sem=sender, recv_sem=receiver,
            device_id=target, device_id_type=MESH,
        )

    def phase1(h):
        return exchange(local.at[h], got1.at[h], send1.at[h], recv1.at[h], across1)

    def phase2(h):
        return exchange(pair.at[h], got2.at[h], send2.at[h], recv2.at[h], across2)

    def phase3(h):
        return exchange(suffix.at[h], got3.at[h], send3.at[h], recv3.at[h], after)

    def id_phase(p):
        target = (across1, across2, after)[p]
        return exchange(id_out.at[p], id_in.at[p], id_send.at[p], id_recv.at[p], target)

    loads[0].wait()
    seg = seg_ref[...].astype(F32)
    first = seg[0:1, 0:1]
    rows = [seg[b:b + 1, :] for b in range(blocks)]
    last = [seg[b:b + 1, STRETCH - 1:STRETCH] for b in range(blocks)]

    id_out[0] = jnp.broadcast_to(last[-1], (8, 128))
    id_phase(0).start()

    odd, top = odd_i.astype(F32), top_i.astype(F32)
    for b in range(blocks):
        grid_rows = jnp.broadcast_to(rows[b], (STRETCH, STRETCH))
        grid_cols = grid_rows.T
        down = lax.broadcasted_iota(jnp.int32, (STRETCH, STRETCH), 0)
        over = lax.broadcasted_iota(jnp.int32, (STRETCH, STRETCH), 1)
        causal[b] = jnp.where(over <= down, same(grid_rows, grid_cols), 0.0)
        causal_t[b] = causal[b].T
        keep[b] = same(grid_cols, first if b == 0 else last[b - 1]).astype(BF16)

    tails = [same(rows[b], last[b]) for b in range(blocks)]

    def columns(h):
        return pl.ds(pl.multiple_of(h * 128, 128), 128)

    def span(b):
        return slice(b * STRETCH, (b + 1) * STRETCH)

    half_down = lax.broadcasted_iota(jnp.int32, (64, 128), 0)
    half_over = lax.broadcasted_iota(jnp.int32, (64, 128), 1)

    def square(packed):
        flat = packed[128:192]
        turned = jnp.concatenate([flat, jnp.zeros_like(flat)], 0).T
        upper = jnp.where(half_down <= half_over, flat, turned[0:64])
        low = jnp.where(half_down > half_over, flat, turned[0:64])
        low = jnp.where(half_down == half_over, packed[192:193], low)
        lower = jnp.where(half_over < 64, turned[64:128], pltpu.roll(low, 64, 1))
        return jnp.concatenate([upper, lower, packed[0:128]], 0)

    def gather_local(h, carry):
        total = jnp.zeros((256, 128), F32)
        for b in range(blocks):
            keys = k_ref[span(b), columns(h)]
            values = v_ref[span(b), columns(h)]
            wide = keys.astype(F32).T
            kt_buf[h, b] = wide.astype(BF16)
            scale = lax.rsqrt(jnp.sum(wide * wide, axis=0, keepdims=True) + 1e-06)
            w1 = memory_row[h, b] * scale
            w2 = w1 * scale
            memory_row[h, b] = w1
            gram_row[h, b] = w2
            ghi, glo = split(wide * (w2 * tails[b]))
            mhi, mlo = split(wide * (w1 * tails[b]))
            gram = mm(jnp.concatenate([ghi, glo], 1), jnp.concatenate([keys, keys], 0))
            memory = mm(jnp.concatenate([mhi, mlo], 1), jnp.concatenate([values, values], 0))
            both = jnp.concatenate([gram, memory], 0)
            if b < blocks - 1:
                part[h, b] = both
            total = total + same(last[b], last[-1]) * both
        low = pltpu.roll(total[64:128], 64, 1)
        local[h, 0:128] = total[128:256]
        local[h, 128:192] = jnp.where(half_down > half_over, low, total[0:64])
        corner = jnp.sum(jnp.where(half_down == half_over, low, 0.0), axis=0, keepdims=True)
        local[h, 192:200] = jnp.broadcast_to(corner, (8, 128))
        phase1(h).start()
        return carry

    for load in loads[1:4]:
        load.wait()
    for h in range(heads):
        for b in range(blocks):
            memory_row[h, b] = gate_ref[h:h + 1, span(b)]
    lax.fori_loop(0, 3, gather_local, 0)
    id_phase(0).wait_recv()
    other_last = id_in[0][0:1, 0:1]
    equal = same(last[-1], other_last)
    pair_local = odd + (1.0 - odd) * equal
    pair_got = (1.0 - odd) + odd * equal
    pair_id = odd * last[-1] + (1.0 - odd) * other_last
    id_out[1] = jnp.broadcast_to(pair_id, (8, 128))
    id_phase(1).start()
    lax.fori_loop(3, 5, gather_local, 0)
    id_phase(1).wait_recv()
    far_id = id_in[1][0:1, 0:1]
    base = top + (1.0 - top) * same(pair_id, far_id)
    suffix_local = base * (odd + (1.0 - odd) * pair_local)
    suffix_got = base * (1.0 - odd) * pair_got
    id_out[2] = jnp.broadcast_to(top * pair_id + (1.0 - top) * far_id, (8, 128))
    id_phase(2).start()

    def solve(base):
        items = [(base + i, b) for i in range(PAIR) for b in range(blocks)]
        every = range(len(items))
        mems, firsts, lows, seconds, weights, held, ridges = [], [], [], [], [], [], []
        xs, rs, ds, sqs = [], [], [], []
        state = None
        for h, b in items:
            if b == 0:
                state = square(in1 * got1[h] + in2 * got2[h] + in3 * got3[h])
            else:
                previous = first if b == 1 else last[b - 2]
                state = part[h, b - 1] + same(last[b - 1], previous) * state
            hi, lo = split(state)
            k = k_ref[span(b), columns(h)]
            v = v_ref[span(b), columns(h)]
            kt = kt_buf[h, b]
            firsts.append(jnp.concatenate([k, hi[:128]], 0))
            lows.append(lo[:128])
            seconds.append(jnp.concatenate([kt, kt], 1))
            mems.append(jnp.concatenate([v, v, hi[128:], hi[128:], lo[128:]], 0))
            column = jnp.broadcast_to(gram_row[h, b], (8, STRETCH)).T[:, 0:1]
            weights.append(causal_t[b] * column)
            held.append(same(rows[b], first if b == 0 else last[b - 1]))
            ridges.append(ridge_ref[h])
            q = q_ref[span(b), columns(h)].astype(F32).T
            q = q * lax.rsqrt(jnp.sum(q * q, axis=0, keepdims=True) + 1e-06)
            rs.append(q)
            ds.append(q)
            sqs.append(jnp.sum(q * q, axis=0, keepdims=True))

        for sweep in range(ITERS - 1):
            cuts = [split(ds[c]) for c in every]
            raised = [
                mm(jnp.concatenate([firsts[c]] * 2, 1), jnp.concatenate(cuts[c], 0)) for c in every
            ]
            lowered = [mm(lows[c], cuts[c][0]) for c in every]
            scores = [split(raised[c][:128] * weights[c]) for c in every]
            inside = [mm(seconds[c], jnp.concatenate(scores[c], 0)) for c in every]
            for c in every:
                d = ds[c]
                image = inside[c] + held[c] * (raised[c][128:] + lowered[c]) + ridges[c] * d
                size = sqs[c] / jnp.sum(d * image, axis=0, keepdims=True)
                if sweep == 0:
                    xs.append(size * d)
                else:
                    xs[c] = xs[c] + size * d
                rs[c] = rs[c] - size * image
                fresh = jnp.sum(rs[c] * rs[c], axis=0, keepdims=True)
                ds[c] = rs[c] + fresh / sqs[c] * d
                sqs[c] = fresh
        raised = [mm(firsts[c], ds[c].astype(BF16)) for c in every]
        for c in every:
            d, scores = ds[c], raised[c][:128]
            form = scores * scores * weights[c] + d * (held[c] * raised[c][128:] + ridges[c] * d)
            xs[c] = xs[c] + sqs[c] / jnp.sum(form, axis=0, keepdims=True) * d

        cuts = [split(xs[c].T) for c in every]
        scores = []
        for c, (h, b) in enumerate(items):
            kt = kt_buf[h, b]
            scores.append(mm(jnp.concatenate(cuts[c], 1), jnp.concatenate([kt, kt], 0)))
        for c, (h, b) in enumerate(items):
            shi, slo = split(scores[c] * (causal[b] * memory_row[h, b]))
            hi, lo = cuts[c]
            mask = keep[b]
            khi, klo = hi * mask, lo * mask
            out = mm(jnp.concatenate([shi, slo, khi, klo, khi], 1), mems[c])
            o_ref[span(b), columns(h)] = out.astype(BF16)

    def relay1(h):
        phase1(h).wait_recv()
        pair[h] = pair_local * local[h] + pair_got * got1[h]
        phase2(h).start()

    def relay2(h):
        phase2(h).wait_recv()
        suffix[h] = (1.0 - top) * got2[h] + suffix_local * local[h] + suffix_got * got1[h]
        phase3(h).start()

    relay1(0)
    lax.fori_loop(5, 8, gather_local, 0)
    relay1(1)
    lax.fori_loop(8, heads, gather_local, 0)
    relay1(2)
    loads[4].wait()
    id_phase(2).wait_recv()
    in1 = odd * same(other_last, first)
    in2 = top * same(far_id, first)
    in3 = same(id_in[2][0:1, 0:1], first)
    relay2(0)
    relay2(1)
    relay1(3)
    groups = heads // PAIR

    def stage(t, carry):
        @pl.when(t < groups - 1)
        def _():
            for i in range(PAIR):
                relay2(PAIR * (t + 1) + i)

        @pl.when(t < groups - 2)
        def _():
            for i in range(PAIR):
                relay1(PAIR * (t + 2) + i)

        for i in range(PAIR):
            phase3(PAIR * t + i).wait_recv()
        solve(PAIR * t)
        return carry

    lax.fori_loop(0, groups, stage, 0)

    def drain(h, carry):
        phase1(h).wait_send()
        phase2(h).wait_send()
        phase3(h).wait_send()
        return carry

    lax.fori_loop(0, heads, drain, 0)
    for p in range(3):
        id_phase(p).wait_send()


def body(sizes, queries, key_vectors, value_vectors, write_gate, ridge_term, segment_ids):
    tokens, width = queries.shape
    heads = ridge_term.shape[0]
    blocks = tokens // STRETCH
    vmem = pl.BlockSpec(memory_space=pltpu.VMEM)
    far = pl.BlockSpec(memory_space=pl.ANY)
    smem = pl.BlockSpec(memory_space=pltpu.SMEM)
    state = pltpu.VMEM((heads, 200, 128), F32)
    return pl.pallas_call(
        functools.partial(kernel, sizes),
        out_shape=jax.ShapeDtypeStruct((tokens, width), BF16),
        in_specs=[far, far, far, far, smem, far],
        out_specs=vmem,
        scratch_shapes=[
            pltpu.VMEM((tokens, width), BF16),
            pltpu.VMEM((tokens, width), BF16),
            pltpu.VMEM((tokens, width), BF16),
            pltpu.VMEM((heads, tokens), F32),
            pltpu.VMEM((blocks, STRETCH), jnp.int32),
            pltpu.SemaphoreType.DMA((5,)),
            pltpu.VMEM((blocks, STRETCH, STRETCH), F32),
            pltpu.VMEM((blocks, STRETCH, STRETCH), F32),
            pltpu.VMEM((blocks, STRETCH, STRETCH), BF16),
            pltpu.VMEM((heads, blocks, 128, STRETCH), BF16),
            pltpu.VMEM((heads, blocks, 1, STRETCH), F32),
            pltpu.VMEM((heads, blocks, 1, STRETCH), F32),
            pltpu.VMEM((heads, blocks - 1, 256, 128), F32),
            state, state, state, state, state, state,
            pltpu.VMEM((3, 8, 128), F32),
            pltpu.VMEM((3, 8, 128), F32),
        ] + [pltpu.SemaphoreType.DMA((heads,))] * 6 + [pltpu.SemaphoreType.DMA((3,))] * 2,
        compiler_params=pltpu.CompilerParams(
            collective_id=0, has_side_effects=True, vmem_limit_bytes=60 * 1024 * 1024
        ),
        cost_estimate=pl.CostEstimate(
            flops=6_000_000_000, bytes_accessed=6_000_000, transcendentals=0
        ),
    )(
        queries, key_vectors, value_vectors, write_gate, ridge_term,
        segment_ids.reshape(blocks, STRETCH),
    )


def solution(mesh):
    sizes = (mesh.shape["outer"], mesh.shape["inner"])
    return jax.shard_map(
        functools.partial(body, sizes),
        mesh=mesh,
        in_specs=(
            P(("outer", "inner"), None),
            P(("outer", "inner"), None),
            P(("outer", "inner"), None),
            P(None, ("outer", "inner")),
            P(),
            P(("outer", "inner")),
        ),
        out_specs=P(("outer", "inner"), None),
        check_vma=False,
    )
```
